256 devices in a mesh: prow: 16 (over x, y), pcol: 16 (over z, core).
Axes of the slice: x: 4, y: 4, z: 8, core: 2. Of those that a mesh axis runs over, the one named last changes fastest.
Arguments:
- inverse_tiles: float32 [24576, 24576], P('prow', 'pcol'), may hold values from -6 to 6
- factor_rows: float32 [24576, 512], P('prow'), may hold values from -0.0390625 to 0.0390625
- diag_inverse: float32 [512, 512], P('prow', 'pcol'), may hold values from -6 to 6
- pattern: int32 [192], replicated, may hold values from 0 to 1, as said below
Outputs:
- column_block: float32 [24576, 512], P(('prow', 'pcol'))
- diagonal_block: float32 [512, 512], P('prow', 'pcol')
The draws below stay inside these ranges and needn't reach their ends.
Inputs may be any that keep to these rules, and one draw needn't show every extreme that they name: `pattern`: 1 where the block of ancestor rows lies in the supernode's structure, else 0; the first block always lies in it and the last never.
All inputs are finite; a program needn't handle non-finite values.
Results may differ from the reference program's by a relative error of at most 0.000078.
Values sent between devices are 32-bit elements; how exact they have to be, the bound alone decides.
A program may use at most 64 MiB of HBM per device.

```python
import jax
import jax.numpy as jnp
from jax import lax

W = 512
BLK = 128
ROWS = 24576
NB = 192


def draw_pattern(key, part):
    first_key = jax.random.fold_in(key, 11)
    second_key = jax.random.fold_in(key, 23)
    group_size = max(1, NB // 16)
    levels = jax.random.randint(first_key, (NB // group_size + 1,), 1, 10)
    block_level = levels[jnp.arange(NB) // group_size]
    draws = jax.random.randint(second_key, (NB,), 0, 10)
    picked = (draws < block_level).astype(jnp.int32)
    picked = picked.at[0].set(1)
    picked = picked.at[NB - 1].set(0)
    return picked


def raised(drawn, rng, source, target, shards_of, factor):
    owner, partner = [(jnp.arange(drawn.shape[axis_at]) // (drawn.shape[axis_at] // shards_of)).reshape([-1 if axis == axis_at else 1 for axis in range(drawn.ndim)]) for axis_at in (source, target)]
    chosen = jax.random.permutation(rng, shards_of)[partner]
    strong = (owner == chosen) | (owner == (partner + shards_of // 2) % shards_of)
    return jnp.where(strong, factor * drawn, drawn)


def steps_of(rng, extent, shards, low, top_value):
    factor_of = 1.0
    for axis_at, shards_of in shards:
        steps = jax.random.uniform(jax.random.fold_in(jax.random.fold_in(rng, 6), axis_at), (shards_of,), jnp.float32, low / len(shards), top_value / len(shards))
        factor_of = factor_of * jnp.repeat(jnp.exp(steps), extent[axis_at] // shards_of).reshape((-1,) + (1,) * (len(extent) - 1 - axis_at))
    return factor_of


def normal_values(stream_key, extent, spread, bound, pieces=(), dtype=jnp.bfloat16):
    values = spread * jax.random.normal(stream_key, extent, jnp.float32)
    if pieces:
        values = values * steps_of(stream_key, extent, pieces, -0.22, 0.18)
    return jnp.clip(values, -bound, bound).astype(dtype)


def noise_with(key, dims, deviation, bound, pieces, heavy, dtype=jnp.bfloat16):
    values = deviation * jax.random.normal(key, dims, jnp.float32)
    if pieces:
        values = values * steps_of(key, dims, pieces, -0.22, 0.18)
    return jnp.clip(raised(values, jax.random.fold_in(key, 3), *heavy), -bound, bound).astype(dtype)


def setup_inputs(seed: int = 0) -> dict:
    arg_keys = jax.random.split(jax.random.key(seed), 5)
    inverse_tiles = noise_with(arg_keys[0], (ROWS, ROWS), 1.0, 6.0, ((0, 16), (1, 16)), (1, 0, 16, 2.0), jnp.float32)
    factor_rows = normal_values(arg_keys[1], (ROWS, W), ROWS ** -0.5, 0.0390625, ((0, 16),), jnp.float32)
    diag_inverse = normal_values(arg_keys[2], (W, W), 1.0, 6.0, ((0, 16), (1, 16)), jnp.float32)
    pattern = draw_pattern(jax.random.fold_in(arg_keys[4], 71), 0)
    return dict(inverse_tiles=inverse_tiles, factor_rows=factor_rows, diag_inverse=diag_inverse, pattern=pattern)


def reference(inverse_tiles, factor_rows, diag_inverse, pattern):
    row_mask = jnp.repeat(pattern, BLK).astype(jnp.float32)
    masked_factor = factor_rows * row_mask[:, None]
    product = jnp.dot(inverse_tiles, masked_factor, precision=lax.Precision.HIGHEST, preferred_element_type=jnp.float32)
    column_block = -product * row_mask[:, None]
    correction = jnp.dot(masked_factor.T, column_block, precision=lax.Precision.HIGHEST, preferred_element_type=jnp.float32)
    diagonal_block = diag_inverse - correction
    return column_block, diagonal_block
```

```python
import jax
import jax.numpy as jnp
from jax import lax
from jax.experimental import pallas as pl
from jax.experimental.pallas import tpu as pltpu
from jax.sharding import PartitionSpec as P

MESH = pl.DeviceIdType.MESH
F32 = jnp.float32
BF16 = jnp.bfloat16

BLK = 128
NX, NY, NZ, NC = 4, 4, 8, 2
NR = NX * NY
NP = NZ * NC
TILE = 1536
SH = TILE // NP
HP = SH // 2
W = 512
WC = 128
NCH = W // WC
DR = W // NR


def split(v):
    hi = v.astype(BF16)
    lo = (v - hi.astype(F32)).astype(BF16)
    return hi, lo


def kernel(
    pat, a_hbm, f_hbm, col_ref, d_ref,
    a32, ahi, alo, fown, fc, fs, pb, xb, zb, dp, db, dz, fthi, ftlo, qs,
    a_sem, f_sem, sc_s, sc_r, own_s, b_s, b_r, c_s, c_r, x_s, x_r, z_s, z_r, d_s, d_r, e_s, e_r,
):
    r = lax.axis_index("prow")
    c = lax.axis_index("pcol")
    x, y = r // NY, r % NY
    z, core = c // NC, c % NC
    is_root = r == c

    def share_of(s):
        h, zz = s // NZ, s % NZ
        dest_core = jnp.where(h == 0, 1 - core, core)
        return NC * zz + dest_core

    def slot_of(share):
        return jnp.where(share % NC == core, NZ, 0) + share // NC

    def f_load(s):
        return pltpu.make_async_copy(f_hbm.at[share_of(s)], fown.at[s], f_sem.at[s])

    def a_load(s):
        return pltpu.make_async_copy(a_hbm.at[share_of(s)], a32.at[s], a_sem.at[s])

    @pl.loop(0, NP)
    def _(s):
        f_load(s).start()

    @pl.loop(0, NP)
    def _(s):
        a_load(s).start()

    barrier = pltpu.get_barrier_semaphore()

    @pl.loop(1, NR)
    def _(k):
        pl.semaphore_signal(barrier, inc=1, device_id=((r + k) % NR, c), device_id_type=MESH)

    @pl.loop(1, NZ)
    def _(k):
        pl.semaphore_signal(barrier, inc=1, device_id=(r, (c + NC * k) % NP), device_id_type=MESH)

    @pl.loop(0, NZ)
    def _(k):
        pl.semaphore_signal(barrier, inc=1, device_id=(r, (NC * ((z + k) % NZ) + 1 - core)), device_id_type=MESH)

    pl.semaphore_wait(barrier, NR - 1 + NZ - 1 + NZ)

    @pl.loop(0, NP)
    def _(s):
        f_load(s).wait()

    def cols(j):
        return pl.ds(j * WC, WC)

    def scatter(j):
        @pl.when(is_root)
        def _():
            @pl.loop(1, NR)
            def _(k):
                to = (r + k) % NR
                pltpu.make_async_remote_copy(
                    src_ref=fown.at[slot_of(to), :, :, cols(j)],
                    dst_ref=fc.at[j, to // NY, to % NY],
                    send_sem=sc_s.at[j], recv_sem=sc_r.at[j],
                    device_id=(to, c), device_id_type=MESH,
                ).start()
            pltpu.make_async_copy(fown.at[slot_of(r), :, :, cols(j)], fc.at[j, x, y], own_s.at[j]).start()

    def scatter_recv(j):
        @pl.when(is_root)
        def _():
            pltpu.make_async_copy(fown.at[slot_of(r), :, :, cols(j)], fc.at[j, x, y], own_s.at[j]).wait()

        @pl.when(jnp.logical_not(is_root))
        def _():
            pltpu.make_async_copy(fc.at[j, x, y], fc.at[j, x, y], sc_r.at[j]).wait()

    def scatter_sent(j):
        @pl.when(is_root)
        def _():
            part = fown.at[pl.ds(0, NR - 1), :, :, cols(j)]
            pltpu.make_async_copy(part, part, sc_s.at[j]).wait()

    def xpeer(k):
        return (((x + k) % NX) * NY + y, c)

    def ypeer(k):
        return (x * NY + (y + k) % NY, c)

    def ring_copies(j, stage):
        ssem, rsem = (b_s, b_r) if stage == 0 else (c_s, c_r)
        out = []
        for k in range(1, 4):
            for h in range(2):
                if stage == 0:
                    mine = fc.at[j, x, y, h]
                elif h == 0:
                    mine = fc.at[j, x, :, 0]
                else:
                    mine = fc.at[j, :, y, 1]
                peer = ypeer(k) if (stage == 0) == (h == 0) else xpeer(k)
                out.append(pltpu.make_async_remote_copy(
                    src_ref=mine, dst_ref=mine, send_sem=ssem.at[j, h, k - 1], recv_sem=rsem.at[j, h, k - 1],
                    device_id=peer, device_id_type=MESH))
        return out

    def ring_send(j, stage):
        for copy in ring_copies(j, stage):
            copy.start()

    def ring_recv(j, stage):
        for copy in ring_copies(j, stage):
            copy.wait_recv()

    def ring_sent(j, stage):
        for copy in ring_copies(j, stage):
            copy.wait_send()

    def split_a(first, last):
        @pl.loop(first, last)
        def _(s):
            a_load(s).wait()

            @pl.loop(0, SH // 16)
            def _(t):
                hi, lo = split(a32[s, pl.ds(pl.multiple_of(t * 16, 16), 16), :])
                rows = pl.ds(pl.multiple_of(s * SH + t * 16, 16), 16)
                ahi[rows, :] = hi
                alo[rows, :] = lo

    def transpose_f():
        for g in range(2):
            masks = []
            for q in range(12):
                row = r * TILE + SH * (NC * (4 * g + q // 3) + core) + 32 * (q % 3)
                masks.append(pat[row // BLK].astype(F32))
            for cb in range(W // 128):
                v = fown[pl.ds(NZ + 4 * g, 4), :, :, pl.ds(cb * 128, 128)].reshape(4 * SH, 128)
                for b in range(3):
                    part = jnp.concatenate(
                        [v[128 * b + 32 * q: 128 * b + 32 * q + 32] * masks[4 * b + q] for q in range(4)], axis=0)
                    hi, lo = split(part.T)
                    at = (pl.ds(cb * 128, 128), pl.ds((3 * g + b) * 128, 128))
                    fthi[at] = hi
                    ftlo[at] = lo

    def split_f(j):
        for xx in range(NX):
            v = fc[j, xx].reshape(NY * SH, WC)
            for b in range(3):
                hi, lo = split(v[b * BLK:(b + 1) * BLK] * pat[c * (TILE // BLK) + 3 * xx + b].astype(F32))
                rows = pl.ds((3 * xx + b) * BLK, BLK)
                fs[rows, 0:WC] = hi
                fs[rows, WC:2 * WC] = lo

    def product(j, h):
        @pl.loop(0, 2)
        def _(t):
            rows = pl.ds(pl.multiple_of(h * NZ * SH + t * 4 * SH, 4 * SH), 4 * SH)
            p = jnp.dot(ahi[rows, :], fs[...], preferred_element_type=F32)
            q = jnp.dot(alo[rows, :], fs[:, 0:WC], preferred_element_type=F32)
            pb[j, h, pl.ds(t * 4, 4)] = (p[:, 0:WC] + (p[:, WC:2 * WC] + q)).reshape(4, SH, WC)

    def exchange(j):
        return pltpu.make_async_remote_copy(
            src_ref=pb.at[j, 0], dst_ref=xb.at[j], send_sem=x_s.at[j], recv_sem=x_r.at[j],
            device_id=(r, c + 1 - 2 * core), device_id_type=MESH)

    def add_exchanged(j):
        exchange(j).wait_recv()
        @pl.loop(0, NZ)
        def _(zz):
            v = pb[j, 1, zz] + xb[j, zz]
            pb[j, 1, zz] = v

    def z_send(j):
        @pl.loop(1, NZ)
        def _(k):
            to = (z + k) % NZ
            pltpu.make_async_remote_copy(
                src_ref=pb.at[j, 1, to], dst_ref=zb.at[j, k - 1], send_sem=z_s.at[j], recv_sem=z_r.at[j],
                device_id=(r, NC * to + core), device_id_type=MESH).start()

    def z_finish(j):
        pltpu.make_async_copy(zb.at[j], zb.at[j], z_r.at[j]).wait()
        total = pb[j, 1, z]
        for k in range(NZ - 1):
            total += zb[j, k]
        for q in range(3):
            row = r * TILE + SH * c + 32 * q
            col_ref[pl.ds(32 * q, 32), cols(j)] = total[32 * q:32 * q + 32] * pat[row // BLK].astype(F32)

    def z_sent(j):
        part = pb.at[j, 1, pl.ds(0, NZ - 1)]
        pltpu.make_async_copy(part, part, z_s.at[j]).wait()

    def diag_product(j):
        for g in range(2):
            v = pb[j, 1, pl.ds(4 * g, 4)].reshape(4 * SH, WC)
            hi, lo = split(v)
            qs[pl.ds(g * 4 * SH, 4 * SH), 0:WC] = hi
            qs[pl.ds(g * 4 * SH, 4 * SH), WC:2 * WC] = lo
        p = jnp.dot(fthi[...], qs[...], preferred_element_type=F32)
        q = jnp.dot(ftlo[...], qs[:, 0:WC], preferred_element_type=F32)
        dp[j] = (p[:, 0:WC] + (p[:, WC:2 * WC] + q)).reshape(NR, DR, WC)

    def d_send(j):
        @pl.loop(1, NR)
        def _(k):
            to = (r + k) % NR
            pltpu.make_async_remote_copy(
                src_ref=dp.at[j, to], dst_ref=db.at[j, k - 1], send_sem=d_s.at[j], recv_sem=d_r.at[j],
                device_id=(to, c), device_id_type=MESH).start()

    def d_sent(j):
        part = dp.at[j, pl.ds(0, NR - 1)]
        pltpu.make_async_copy(part, part, d_s.at[j]).wait()

    def e_copy(j, dest):
        return pltpu.make_async_remote_copy(
            src_ref=db.at[j, NR - 1], dst_ref=dz.at[c], send_sem=e_s.at[j, dest], recv_sem=e_r.at[c],
            device_id=(r, 4 * j + dest), device_id_type=MESH)

    def d_finish(j):
        pltpu.make_async_copy(db.at[j, pl.ds(0, NR - 1)], db.at[j, pl.ds(0, NR - 1)], d_r.at[j]).wait()
        total = dp[j, r]
        for k in range(NR - 1):
            total += db[j, k]
        db[j, NR - 1] = total
        for dest in range(4):
            @pl.when(c != 4 * j + dest)
            def _():
                e_copy(j, dest).start()

        @pl.when(c // 4 == j)
        def _():
            dz[c] = total

    def e_sent(j):
        for dest in range(4):
            @pl.when(c != 4 * j + dest)
            def _():
                e_copy(j, dest).wait_send()

    for j in range(NCH):
        scatter(j)

    def relay(step):
        if 0 <= step - 1 < NCH:
            ring_recv(step - 1, 0)
            ring_send(step - 1, 1)
        if step < NCH:
            scatter_recv(step)
            ring_send(step, 0)

    def compute(j):
        ring_recv(j, 1)
        split_f(j)
        product(j, 0)
        exchange(j).start()
        product(j, 1)

    def reduce(j):
        add_exchanged(j)
        z_send(j)
        diag_product(j)
        d_send(j)

    def finish(j):
        d_finish(j)
        z_finish(j)

    split_a(0, 4)
    relay(0)
    split_a(4, 10)
    relay(1)
    split_a(10, 16)
    transpose_f()
    relay(2)
    for j in range(NCH):
        compute(j)
        relay(j + 3)
        reduce(j)
        if j >= 1:
            finish(j - 1)
    for j in range(NCH):
        scatter_sent(j)
        ring_sent(j, 0)
        ring_sent(j, 1)
        exchange(j).wait_send()
    finish(NCH - 1)
    for j in range(NCH):
        z_sent(j)
        d_sent(j)
        e_sent(j)

    for k in range(1, NP):
        src = (c + k) % NP
        pltpu.make_async_copy(dz.at[src], dz.at[src], e_r.at[src]).wait()
    total = dz[0]
    for k in range(1, NP):
        total += dz[k]
    d_ref[...] = total


def local(inverse_tiles, factor_rows, diag_inverse, pattern):
    c = lax.axis_index("pcol")
    dma = pltpu.SemaphoreType.DMA
    col, d = pl.pallas_call(
        kernel,
        out_shape=(jax.ShapeDtypeStruct((SH, W), F32), jax.ShapeDtypeStruct((DR, WC), F32)),
        in_specs=[
            pl.BlockSpec(memory_space=pltpu.SMEM),
            pl.BlockSpec(memory_space=pl.ANY),
            pl.BlockSpec(memory_space=pl.ANY),
        ],
        out_specs=(pl.BlockSpec(memory_space=pltpu.VMEM), pl.BlockSpec(memory_space=pltpu.VMEM)),
        scratch_shapes=[
            pltpu.VMEM((NP, SH, TILE), F32),
            pltpu.VMEM((TILE, TILE), BF16),
            pltpu.VMEM((TILE, TILE), BF16),
            pltpu.VMEM((NP, 2, HP, W), F32),
            pltpu.VMEM((NCH, NX, NY, 2, HP, WC), F32),
            pltpu.VMEM((TILE, 2 * WC), BF16),
            pltpu.VMEM((NCH, 2, NZ, SH, WC), F32),
            pltpu.VMEM((NCH, NZ, SH, WC), F32),
            pltpu.VMEM((NCH, NZ - 1, SH, WC), F32),
            pltpu.VMEM((NCH, NR, DR, WC), F32),
            pltpu.VMEM((NCH, NR, DR, WC), F32),
            pltpu.VMEM((NP, DR, WC), F32),
            pltpu.VMEM((W, NZ * SH), BF16),
            pltpu.VMEM((W, NZ * SH), BF16),
            pltpu.VMEM((NZ * SH, 2 * WC), BF16),
            dma((NP,)), dma((NP,)),
            dma((NCH,)), dma((NCH,)), dma((NCH,)),
            dma((NCH, 2, 3)), dma((NCH, 2, 3)),
            dma((NCH, 2, 3)), dma((NCH, 2, 3)),
            dma((NCH,)), dma((NCH,)),
            dma((NCH,)), dma((NCH,)),
            dma((NCH,)), dma((NCH,)),
            dma((NCH, 4)), dma((NP,)),
        ],
        compiler_params=pltpu.CompilerParams(collective_id=1, has_side_effects=True, vmem_limit_bytes=60 << 20),
        name="selected_inversion",
    )(pattern, inverse_tiles.reshape(NP, SH, TILE), factor_rows.reshape(NP, 2, HP, W))
    mine = lax.dynamic_slice_in_dim(d, (c % 4) * DR, DR, 1)
    return -col, diag_inverse + mine


def solution(mesh):
    return jax.shard_map(
        local,
        mesh=mesh,
        in_specs=(P("prow", "pcol"), P("prow", None), P("prow", "pcol"), P()),
        out_specs=(P(("prow", "pcol"), None), P("prow", "pcol")),
        check_vma=False,
    )
```

```python
import jax
import jax.numpy as jnp
from jax import lax
from jax.experimental import pallas as pl
from jax.experimental.pallas import tpu as pltpu
from jax.sharding import PartitionSpec as P

MESH = pl.DeviceIdType.MESH
F32 = jnp.float32
BF16 = jnp.bfloat16

BLK = 128
NX, NY, NZ, NC = 4, 4, 8, 2
NR = NX * NY
NP = NZ * NC
TILE = 1536
SH = TILE // NP
HP = SH // 2
W = 512
WC = 128
NCH = W // WC
DR = W // NR


DIRS = ((1, 0), (3, 0), (0, 1), (0, 3))
SEND = ((57344, 24321, 12544, 4352), (4017, 224, 560, 16), (8, 32776, 34944, 52429), (70, 8198, 17479, 8736))
DEPTH = ((23130, 60186, 1252), (23130, 7146, 58372), (23130, 55510, 10016), (23130, 29308, 36224))
QR = TILE // 4
NSUB = 2
SR = QR // NSUB
NS = NCH * NSUB
HOP = 3
PRE = 7
GROUPS = ((0, 1, 2), (3,))
ZCOPIES = (
    (-1, -3, 0, SH), (-2, -4, 0, HP), (1, 3, 0, SH), (2, 4, HP, HP),
    (-1, -1, 0, SH), (1, 1, 0, SH), (-2, -2, 0, SH), (2, 2, 0, SH),
)
XYORDER = ((2, 2), (1, 0), (3, 0), (0, 1), (0, 3), (1, 1), (3, 3), (1, 3), (3, 1), (2, 0), (0, 2), (2, 1), (1, 2), (2, 3), (3, 2))


def split(v):
    hi = v.astype(BF16)
    lo = (v - hi.astype(F32)).astype(BF16)
    return hi, lo


def kernel(
    pat, a_hbm, f_hbm, col_ref, d_ref,
    a32, ahi, alo, fown, fc, fs, pb, xb, zb, dp, db, dz, fthi, ftlo, qs,
    a_sem, f_sem, own_s, t_s, t_r, x_s, x_r, z_s, z_r, d_s, d_r, e_s, e_r,
):
    r = lax.axis_index("prow")
    c = lax.axis_index("pcol")
    x, y = r // NY, r % NY
    z, core = c // NC, c % NC
    is_root = r == c

    def share_of(s):
        h, zz = s // NZ, s % NZ
        dest_core = jnp.where(h == 0, 1 - core, core)
        return NC * zz + dest_core

    def f_load(s):
        return pltpu.make_async_copy(f_hbm.at[pl.ds(pl.multiple_of((NC * s + core) * SH, 8), SH)], fown.at[s], f_sem.at[s])

    def a_load(s):
        return pltpu.make_async_copy(a_hbm.at[share_of(s)], a32.at[s], a_sem.at[s])

    def root_load(j):
        return pltpu.make_async_copy(f_hbm.at[:, cols(j)], fc.at[j], own_s.at[j])

    def cols(j):
        return pl.ds(j * WC, WC)

    @pl.when(is_root)
    def _():
        for j in range(NCH):
            root_load(j).start()

    @pl.loop(0, NP)
    def _(s):
        a_load(s).start()

    for zz in range(NZ):
        f_load(zz).start()

    barrier = pltpu.get_barrier_semaphore()
    for dx, dy in XYORDER:
        pl.semaphore_signal(
            barrier, inc=1, device_id=((x + dx) % NX * NY + (y + dy) % NY, c), device_id_type=MESH)

    @pl.loop(1, NP)
    def _(k):
        pl.semaphore_signal(barrier, inc=1, device_id=(r, (c + k) % NP), device_id_type=MESH)

    root_x, root_y = c // NY, c % NY
    pos = (x - root_x + NX) % NX * NY + (y - root_y + NY) % NY
    depth = [sum(((DEPTH[t][k] >> pos) & 1) << k for k in range(3)) for t in range(4)]
    sends = [[(SEND[t][d] >> pos) & 1 for d in range(4)] for t in range(4)]
    rank = [sum((((depth[u] < depth[t]) | ((depth[u] == depth[t]) & (u < t))).astype(jnp.int32) for u in range(4) if u != t), 0) for t in range(4)]
    order = [sum(t * (rank[t] == k).astype(jnp.int32) for t in range(4)) for k in range(4)]
    peers = [((x + dx) % NX * NY + (y + dy) % NY, c) for dx, dy in DIRS]

    def piece(t, s):
        return fc.at[s // NSUB, pl.ds(pl.multiple_of(t * QR + (s % NSUB) * SR, 8), SR)]

    def tree_copy(t, s, d):
        return pltpu.make_async_remote_copy(
            src_ref=piece(t, s), dst_ref=piece(t, s), send_sem=t_s.at[t, d], recv_sem=t_r.at[t, s],
            device_id=peers[d], device_id_type=MESH)

    def tree_send(t, s):
        for d in range(4):
            @pl.when(sends[t][d] == 1)
            def _():
                tree_copy(t, s, d).start()

    def relay(n):
        for t in range(4):
            s = jnp.where(is_root, n, n - HOP * (depth[t] - 1))

            @pl.when((s >= 0) & (s < NS))
            def _():
                @pl.when(jnp.logical_not(is_root))
                def _():
                    pltpu.make_async_copy(piece(t, s), piece(t, s), t_r.at[t, s]).wait()
                tree_send(t, s)

    def tree_sent():
        for t in range(4):
            part = fc.at[:, pl.ds(t * QR, QR)]
            for d in range(4):
                @pl.when(sends[t][d] == 1)
                def _():
                    pltpu.make_async_copy(part, part, t_s.at[t, d]).wait()

    def split_a(first, last):
        @pl.loop(first, last)
        def _(s):
            for k in range(4):
                hi, lo = split(a32[s, :, pl.ds(pl.multiple_of(order[k] * QR, 128), QR)])
                at = (pl.ds(pl.multiple_of(s * SH, 16), SH), pl.ds(k * QR, QR))
                ahi[at] = hi
                alo[at] = lo

    def a_wait(first, last):
        @pl.loop(first, last)
        def _(s):
            a_load(s).wait()

    def transpose_f():
        for g in range(2):
            masks = []
            for q in range(12):
                row = r * TILE + SH * (NC * (4 * g + q // 3) + core) + 32 * (q % 3)
                masks.append(pat[row // BLK].astype(F32))
            for cb in range(W // 128):
                v = fown[pl.ds(4 * g, 4), :, pl.ds(cb * 128, 128)].reshape(4 * SH, 128)
                for b in range(3):
                    part = jnp.concatenate(
                        [v[128 * b + 32 * q: 128 * b + 32 * q + 32] * masks[4 * b + q] for q in range(4)], axis=0)
                    hi, lo = split(part.T)
                    at = (pl.ds(cb * 128, 128), pl.ds((3 * g + b) * 128, 128))
                    fthi[at] = hi
                    ftlo[at] = lo

    def split_f(j, pair):
        for k in (2 * pair, 2 * pair + 1):
            for b in range(QR // BLK):
                rows = pl.ds(pl.multiple_of(order[k] * QR + b * BLK, BLK), BLK)
                hi, lo = split(fc[j, rows] * pat[c * (TILE // BLK) + order[k] * (QR // BLK) + b].astype(F32))
                rows = pl.ds(k * QR + b * BLK, BLK)
                fs[rows, 0:WC] = hi
                fs[rows, WC:2 * WC] = lo

    def product(j, h, pair):
        rows, depths = pl.ds(h * NZ * SH, NZ * SH), pl.ds(pair * 2 * QR, 2 * QR)
        p = jnp.dot(ahi[rows, depths], fs[depths, :], preferred_element_type=F32)
        q = jnp.dot(alo[rows, depths], fs[depths, 0:WC], preferred_element_type=F32)
        v = (p[:, 0:WC] + (p[:, WC:2 * WC] + q)).reshape(NZ, SH, WC)
        pb[j, h] = v if pair == 0 else pb[j, h] + v

    def exchange(j):
        return pltpu.make_async_remote_copy(
            src_ref=pb.at[j, 0], dst_ref=xb.at[j], send_sem=x_s.at[j], recv_sem=x_r.at[j],
            device_id=(r, c + 1 - 2 * core), device_id_type=MESH)

    def ex_send(j):
        exchange(j).start()

    def ex_recv(j):
        exchange(j).wait_recv()

    def ex_sent(j):
        exchange(j).wait_send()

    def add_exchanged(j):
        @pl.loop(0, NZ)
        def _(zz):
            v = pb[j, 1, zz] + xb[j, zz]
            pb[j, 1, zz] = v

    def z_copy(j, slot):
        away, off, first, count = ZCOPIES[slot]
        rows = pl.ds(first, count)
        return pltpu.make_async_remote_copy(
            src_ref=pb.at[j, 1, (z + off + NZ) % NZ, rows], dst_ref=zb.at[j, slot, rows],
            send_sem=z_s.at[j], recv_sem=z_r.at[j, slot // 4],
            device_id=(r, (c + NC * away + NP) % NP), device_id_type=MESH)

    def z_send(j, slot):
        z_copy(j, slot).start()

    def z_recv(j, stage):
        part = zb.at[j, pl.ds(4 * stage, 3 + stage)]
        pltpu.make_async_copy(part, part, z_r.at[j, stage]).wait()

    def z_sent(j):
        part = zb.at[j, pl.ds(0, 7)]
        pltpu.make_async_copy(part, part, z_s.at[j]).wait()

    def z_add(j):
        for slot in range(4):
            _, _, first, count = ZCOPIES[slot]
            share, rows = (z + (NZ - 2 if slot < 2 else 2)) % NZ, pl.ds(first, count)
            pb[j, 1, share, rows] = pb[j, 1, share, rows] + zb[j, slot, rows]

    def z_first(j):
        for slot in (1, 3, 0, 2, 4, 5):
            z_send(j, slot)

    def z_second(j):
        z_recv(j, 0)
        z_add(j)
        for slot in (6, 7):
            z_send(j, slot)

    def z_finish(j):
        z_recv(j, 1)
        total = pb[j, 1, z] + ((zb[j, 4] + zb[j, 5]) + (zb[j, 6] + zb[j, 7]))
        for q in range(3):
            row = r * TILE + SH * c + 32 * q
            col_ref[pl.ds(32 * q, 32), cols(j)] = total[32 * q:32 * q + 32] * pat[row // BLK].astype(F32)

    def diag_product(j):
        for g in range(2):
            v = pb[j, 1, pl.ds(4 * g, 4)].reshape(4 * SH, WC)
            hi, lo = split(v)
            qs[pl.ds(g * 4 * SH, 4 * SH), 0:WC] = hi
            qs[pl.ds(g * 4 * SH, 4 * SH), WC:2 * WC] = lo
        p = jnp.dot(fthi[...], qs[...], preferred_element_type=F32)
        q = jnp.dot(ftlo[...], qs[:, 0:WC], preferred_element_type=F32)
        dp[:, :, cols(j)] = (p[:, 0:WC] + (p[:, WC:2 * WC] + q)).reshape(NR, DR, WC)

    def d_cols(g):
        return pl.ds(GROUPS[g][0] * WC, len(GROUPS[g]) * WC)

    def d_send(g):
        for k, (dx, dy) in enumerate(XYORDER, 1):
            to = (x + dx) % NX * NY + (y + dy) % NY
            pltpu.make_async_remote_copy(
                src_ref=dp.at[to, :, d_cols(g)], dst_ref=db.at[k - 1, :, d_cols(g)],
                send_sem=d_s.at[g], recv_sem=d_r.at[g],
                device_id=(to, c), device_id_type=MESH).start()

    def d_sent(g):
        part = dp.at[pl.ds(0, NR - 1), :, d_cols(g)]
        pltpu.make_async_copy(part, part, d_s.at[g]).wait()

    def e_copy(j, dest):
        return pltpu.make_async_remote_copy(
            src_ref=db.at[NR - 1, :, cols(j)], dst_ref=dz.at[c], send_sem=e_s.at[j], recv_sem=e_r.at[0],
            device_id=(r, 4 * j + dest), device_id_type=MESH)

    def d_recv(g):
        part = db.at[pl.ds(0, NR - 1), :, d_cols(g)]
        pltpu.make_async_copy(part, part, d_r.at[g]).wait()

    def e_send(j):
        for dest in range(4):
            @pl.when(c != 4 * j + dest)
            def _():
                e_copy(j, dest).start()

    def d_finish(g):
        d_recv(g)
        total = dp[r, :, d_cols(g)]
        for k in range(NR - 1):
            total += db[k, :, d_cols(g)]
        db[NR - 1, :, d_cols(g)] = total
        for i, j in enumerate(GROUPS[g]):
            e_send(j)

            @pl.when(c // 4 == j)
            def _():
                dz[c] = total[:, i * WC:(i + 1) * WC]

    def e_sent(j):
        pltpu.make_async_copy(dz.at[pl.ds(0, 3)], dz.at[pl.ds(0, 3)], e_s.at[j]).wait()

        @pl.when(c // 4 != j)
        def _():
            pltpu.make_async_copy(dz.at[0], dz.at[0], e_s.at[j]).wait()

    def e_recv():
        part = dz.at[pl.ds(0, NP - 1)]
        pltpu.make_async_copy(part, part, e_r.at[0]).wait()

    def early(j):
        split_f(j, 0)
        product(j, 0, 0)
        product(j, 1, 0)

    def late(j):
        split_f(j, 1)
        product(j, 0, 1)
        ex_send(j)
        product(j, 1, 1)

    def exchanged(j):
        ex_recv(j)
        add_exchanged(j)
        z_first(j)

    a_wait(0, PRE)
    split_a(0, PRE)
    pl.semaphore_wait(barrier, NR - 1 + NP - 1)

    @pl.when(is_root)
    def _():
        for j in range(NCH):
            root_load(j).wait()

    @pl.loop(0, 10)
    def _(n):
        relay(n)

        @pl.when(n < NP - PRE)
        def _():
            a_wait(n + PRE, n + PRE + 1)
            split_a(n + PRE, n + PRE + 1)

        @pl.when(n == NP - PRE)
        def _():
            for zz in range(NZ):
                f_load(zz).wait()
            transpose_f()

    relay(10)
    early(0)
    relay(11)
    relay(12)
    early(1)
    relay(13)
    late(0)
    relay(14)
    early(2)
    exchanged(0)
    relay(15)
    late(1)
    relay(16)
    early(3)
    exchanged(1)
    relay(17)
    late(2)
    diag_product(0)
    relay(18)
    exchanged(2)
    z_second(0)
    diag_product(1)
    z_second(1)
    diag_product(2)
    d_send(0)
    relay(19)
    late(3)
    exchanged(3)
    diag_product(3)
    d_send(1)
    z_second(2)
    z_second(3)
    tree_sent()
    d_finish(0)
    z_finish(0)
    d_finish(1)
    z_finish(1)
    z_finish(2)
    for j in range(NCH):
        ex_sent(j)
        z_sent(j)
    z_finish(3)
    for j in range(NCH):
        e_sent(j)
    for g in range(2):
        d_sent(g)
    e_recv()
    total = dz[0]
    for k in range(1, NP):
        total += dz[k]
    d_ref[...] = total


def local(inverse_tiles, factor_rows, diag_inverse, pattern):
    c = lax.axis_index("pcol")
    dma = pltpu.SemaphoreType.DMA
    col, d = pl.pallas_call(
        kernel,
        out_shape=(jax.ShapeDtypeStruct((SH, W), F32), jax.ShapeDtypeStruct((DR, WC), F32)),
        in_specs=[
            pl.BlockSpec(memory_space=pltpu.SMEM),
            pl.BlockSpec(memory_space=pl.ANY),
            pl.BlockSpec(memory_space=pl.ANY),
        ],
        out_specs=(pl.BlockSpec(memory_space=pltpu.VMEM), pl.BlockSpec(memory_space=pltpu.VMEM)),
        scratch_shapes=[
            pltpu.VMEM((NP, SH, TILE), F32),
            pltpu.VMEM((TILE, TILE), BF16),
            pltpu.VMEM((TILE, TILE), BF16),
            pltpu.VMEM((NZ, SH, W), F32),
            pltpu.VMEM((NCH, TILE, WC), F32),
            pltpu.VMEM((TILE, 2 * WC), BF16),
            pltpu.VMEM((NCH, 2, NZ, SH, WC), F32),
            pltpu.VMEM((NCH, NZ, SH, WC), F32),
            pltpu.VMEM((NCH, 8, SH, WC), F32),
            pltpu.VMEM((NR, DR, W), F32),
            pltpu.VMEM((NR, DR, W), F32),
            pltpu.VMEM((NP, DR, WC), F32),
            pltpu.VMEM((W, NZ * SH), BF16),
            pltpu.VMEM((W, NZ * SH), BF16),
            pltpu.VMEM((NZ * SH, 2 * WC), BF16),
            dma((NP,)), dma((NZ,)),
            dma((NCH,)), dma((4, 4)), dma((4, NS)),
            dma((NCH,)), dma((NCH,)),
            dma((NCH,)), dma((NCH, 2)),
            dma((2,)), dma((2,)),
            dma((NCH,)), dma((1,)),
        ],
        compiler_params=pltpu.CompilerParams(collective_id=1, has_side_effects=True, vmem_limit_bytes=60 << 20),
        name="selected_inversion",
    )(pattern, inverse_tiles.reshape(NP, SH, TILE), factor_rows)
    mine = lax.dynamic_slice_in_dim(d, (c % 4) * DR, DR, 1)
    return -col, diag_inverse + mine


def solution(mesh):
    return jax.shard_map(
        local,
        mesh=mesh,
        in_specs=(P("prow", "pcol"), P("prow", None), P("prow", "pcol"), P()),
        out_specs=(P(("prow", "pcol"), None), P("prow", "pcol")),
        check_vma=False,
    )
```

```python
import jax
import jax.numpy as jnp
from jax import lax
from jax.experimental import pallas as pl
from jax.experimental.pallas import tpu as pltpu
from jax.sharding import PartitionSpec as P

MESH = pl.DeviceIdType.MESH
F32 = jnp.float32
BF16 = jnp.bfloat16

BLK = 128
NX, NY, NZ, NC = 4, 4, 8, 2
NR = NX * NY
NP = NZ * NC
TILE = 1536
SH = TILE // NP
HP = SH // 2
W = 512
WC = 128
NCH = W // WC
DR = W // NR


DIRS = ((1, 0), (3, 0), (0, 1), (0, 3))
SEND = ((57344, 24321, 12544, 4352), (4017, 224, 560, 16), (8, 32776, 34944, 52429), (70, 8198, 17479, 8736))
DEPTH = ((23130, 60186, 1252), (23130, 7146, 58372), (23130, 55510, 10016), (23130, 29308, 36224))
QR = TILE // 4
NSUB = 2
SR = QR // NSUB
NS = NCH * NSUB
HOP = 3
PRE = 7
GROUPS = ((0, 1, 2), (3,))
ZCOPIES = (
    (-1, -3, 0, SH), (-2, -4, 0, HP), (1, 3, 0, SH), (2, 4, HP, HP),
    (-1, -1, 0, SH), (1, 1, 0, SH), (-2, -2, 0, SH), (2, 2, 0, SH),
)
XYORDER = ((2, 2), (1, 0), (3, 0), (0, 1), (0, 3), (1, 1), (3, 3), (1, 3), (3, 1), (2, 0), (0, 2), (2, 1), (1, 2), (2, 3), (3, 2))


def split(v):
    hi = v.astype(BF16)
    lo = (v - hi.astype(F32)).astype(BF16)
    return hi, lo


def kernel(
    pat, a_hbm, f_hbm, col_ref, d_ref,
    a32, ahi, alo, fown, fc, fs, pb, xb, zb, dp, db, dz, fthi, ftlo, qs,
    a_sem, f_sem, own_s, t_s, t_r, x_s, x_r, z_s, z_r, d_s, d_r, e_s, e_r,
):
    r = lax.axis_index("prow")
    c = lax.axis_index("pcol")
    x, y = r >> 2, r & (NY - 1)
    z, core = c >> 1, c & (NC - 1)
    is_root = r == c

    def share_of(s):
        h, zz = s >> 3, s & (NZ - 1)
        dest_core = jnp.where(h == 0, 1 - core, core)
        return NC * zz + dest_core

    def f_load(s):
        return pltpu.make_async_copy(f_hbm.at[pl.ds(pl.multiple_of((NC * s + core) * SH, 8), SH)], fown.at[s], f_sem.at[s])

    def a_load(s):
        return pltpu.make_async_copy(a_hbm.at[share_of(s)], a32.at[s], a_sem.at[s])

    def root_load(j):
        return pltpu.make_async_copy(f_hbm.at[:, cols(j)], fc.at[j], own_s.at[j])

    def cols(j):
        return pl.ds(j * WC, WC)

    @pl.when(is_root)
    def _():
        for j in range(NCH):
            root_load(j).start()

    @pl.loop(0, NP)
    def _(s):
        a_load(s).start()

    for zz in range(NZ):
        f_load(zz).start()

    barrier = pltpu.get_barrier_semaphore()
    for dx, dy in XYORDER:
        pl.semaphore_signal(
            barrier, inc=1, device_id=(((x + dx) & (NX - 1)) * NY + ((y + dy) & (NY - 1)), c), device_id_type=MESH)

    @pl.loop(1, NP)
    def _(k):
        pl.semaphore_signal(barrier, inc=1, device_id=(r, (c + k) & (NP - 1)), device_id_type=MESH)

    root_x, root_y = c >> 2, c & (NY - 1)
    pos = ((x - root_x + NX) & (NX - 1)) * NY + ((y - root_y + NY) & (NY - 1))
    depth = [sum(((DEPTH[t][k] >> pos) & 1) << k for k in range(3)) for t in range(4)]
    sends = [[(SEND[t][d] >> pos) & 1 for d in range(4)] for t in range(4)]
    rank = [sum((((depth[u] < depth[t]) | ((depth[u] == depth[t]) & (u < t))).astype(jnp.int32) for u in range(4) if u != t), 0) for t in range(4)]
    order = [sum(t * (rank[t] == k).astype(jnp.int32) for t in range(4)) for k in range(4)]
    peers = [(((x + dx) & (NX - 1)) * NY + ((y + dy) & (NY - 1)), c) for dx, dy in DIRS]

    def piece(t, s):
        return fc.at[s >> 1, pl.ds(pl.multiple_of(t * QR + (s & (NSUB - 1)) * SR, 8), SR)]

    def tree_copy(t, s, d):
        return pltpu.make_async_remote_copy(
            src_ref=piece(t, s), dst_ref=piece(t, s), send_sem=t_s.at[t, d], recv_sem=t_r.at[t, s],
            device_id=peers[d], device_id_type=MESH)

    def tree_send(t, s):
        for d in range(4):
            @pl.when(sends[t][d] == 1)
            def _():
                tree_copy(t, s, d).start()

    def root_send():
        for j in range(NCH):
            root_load(j).wait()

            @pl.loop(j * NSUB, (j + 1) * NSUB)
            def _(s):
                for t in range(4):
                    tree_send(t, s)

    def relay(n):
        for t in range(4):
            s = n - HOP * (depth[t] - 1)

            @pl.when(jnp.logical_not(is_root) & (s >= 0) & (s < NS))
            def _():
                pltpu.make_async_copy(piece(t, s), piece(t, s), t_r.at[t, s]).wait()
                tree_send(t, s)

    def tree_sent():
        for t in range(4):
            part = fc.at[:, pl.ds(t * QR, QR)]
            for d in range(4):
                @pl.when(sends[t][d] == 1)
                def _():
                    pltpu.make_async_copy(part, part, t_s.at[t, d]).wait()

    def split_a(first, last):
        @pl.loop(first, last)
        def _(s):
            for k in range(4):
                hi, lo = split(a32[s, :, pl.ds(pl.multiple_of(order[k] * QR, 128), QR)])
                at = (pl.ds(pl.multiple_of(s * SH, 16), SH), pl.ds(k * QR, QR))
                ahi[at] = hi
                alo[at] = lo

    def a_wait(first, last):
        @pl.loop(first, last)
        def _(s):
            a_load(s).wait()

    def transpose_f():
        for g in range(2):
            masks = []
            for q in range(12):
                row = r * TILE + SH * (NC * (4 * g + q // 3) + core) + 32 * (q % 3)
                masks.append(pat[row >> 7].astype(F32))
            for cb in range(W // 128):
                v = fown[pl.ds(4 * g, 4), :, pl.ds(cb * 128, 128)].reshape(4 * SH, 128)
                for b in range(3):
                    part = jnp.concatenate(
                        [v[128 * b + 32 * q: 128 * b + 32 * q + 32] * masks[4 * b + q] for q in range(4)], axis=0)
                    hi, lo = split(part.T)
                    at = (pl.ds(cb * 128, 128), pl.ds((3 * g + b) * 128, 128))
                    fthi[at] = hi
                    ftlo[at] = lo

    def split_f(j, pair):
        for k in (2 * pair, 2 * pair + 1):
            for b in range(QR // BLK):
                rows = pl.ds(pl.multiple_of(order[k] * QR + b * BLK, BLK), BLK)
                hi, lo = split(fc[j, rows] * pat[c * (TILE // BLK) + order[k] * (QR // BLK) + b].astype(F32))
                rows = pl.ds(k * QR + b * BLK, BLK)
                fs[rows, 0:WC] = hi
                fs[rows, WC:2 * WC] = lo

    def product(j, h, pair):
        rows, depths = pl.ds(h * NZ * SH, NZ * SH), pl.ds(pair * 2 * QR, 2 * QR)
        p = jnp.dot(ahi[rows, depths], fs[depths, :], preferred_element_type=F32)
        q = jnp.dot(alo[rows, depths], fs[depths, 0:WC], preferred_element_type=F32)
        v = (p[:, 0:WC] + (p[:, WC:2 * WC] + q)).reshape(NZ, SH, WC)
        pb[j, h] = v if pair == 0 else pb[j, h] + v

    def exchange(j):
        return pltpu.make_async_remote_copy(
            src_ref=pb.at[j, 0], dst_ref=xb.at[j], send_sem=x_s.at[j], recv_sem=x_r.at[j],
            device_id=(r, c + 1 - 2 * core), device_id_type=MESH)

    def ex_send(j):
        exchange(j).start()

    def ex_recv(j):
        exchange(j).wait_recv()

    def ex_sent(j):
        exchange(j).wait_send()

    def add_exchanged(j):
        @pl.loop(0, NZ)
        def _(zz):
            v = pb[j, 1, zz] + xb[j, zz]
            pb[j, 1, zz] = v

    def z_copy(j, slot):
        away, off, first, count = ZCOPIES[slot]
        rows = pl.ds(first, count)
        return pltpu.make_async_remote_copy(
            src_ref=pb.at[j, 1, (z + off + NZ) & (NZ - 1), rows], dst_ref=zb.at[j, slot, rows],
            send_sem=z_s.at[j], recv_sem=z_r.at[j, slot // 4],
            device_id=(r, (c + NC * away + NP) & (NP - 1)), device_id_type=MESH)

    def z_send(j, slot):
        z_copy(j, slot).start()

    def z_recv(j, stage):
        part = zb.at[j, pl.ds(4 * stage, 3 + stage)]
        pltpu.make_async_copy(part, part, z_r.at[j, stage]).wait()

    def z_sent(j):
        part = zb.at[j, pl.ds(0, 7)]
        pltpu.make_async_copy(part, part, z_s.at[j]).wait()

    def z_add(j):
        for slot in range(4):
            _, _, first, count = ZCOPIES[slot]
            share, rows = (z + (NZ - 2 if slot < 2 else 2)) & (NZ - 1), pl.ds(first, count)
            pb[j, 1, share, rows] = pb[j, 1, share, rows] + zb[j, slot, rows]

    def z_first(j):
        for slot in (1, 3, 0, 2, 4, 5):
            z_send(j, slot)

    def z_second(j):
        z_recv(j, 0)
        z_add(j)
        for slot in (6, 7):
            z_send(j, slot)

    def z_finish(j):
        z_recv(j, 1)
        total = pb[j, 1, z] + ((zb[j, 4] + zb[j, 5]) + (zb[j, 6] + zb[j, 7]))
        for q in range(3):
            row = r * TILE + SH * c + 32 * q
            col_ref[pl.ds(32 * q, 32), cols(j)] = total[32 * q:32 * q + 32] * pat[row >> 7].astype(F32)

    def diag_product(j):
        for g in range(2):
            v = pb[j, 1, pl.ds(4 * g, 4)].reshape(4 * SH, WC)
            hi, lo = split(v)
            qs[pl.ds(g * 4 * SH, 4 * SH), 0:WC] = hi
            qs[pl.ds(g * 4 * SH, 4 * SH), WC:2 * WC] = lo
        p = jnp.dot(fthi[...], qs[...], preferred_element_type=F32)
        q = jnp.dot(ftlo[...], qs[:, 0:WC], preferred_element_type=F32)
        dp[:, :, cols(j)] = (p[:, 0:WC] + (p[:, WC:2 * WC] + q)).reshape(NR, DR, WC)

    def d_cols(g):
        return pl.ds(GROUPS[g][0] * WC, len(GROUPS[g]) * WC)

    def d_send(g):
        for k, (dx, dy) in enumerate(XYORDER, 1):
            to = ((x + dx) & (NX - 1)) * NY + ((y + dy) & (NY - 1))
            pltpu.make_async_remote_copy(
                src_ref=dp.at[to, :, d_cols(g)], dst_ref=db.at[k - 1, :, d_cols(g)],
                send_sem=d_s.at[g], recv_sem=d_r.at[g],
                device_id=(to, c), device_id_type=MESH).start()

    def d_sent(g):
        part = dp.at[pl.ds(0, NR - 1), :, d_cols(g)]
        pltpu.make_async_copy(part, part, d_s.at[g]).wait()

    def e_copy(j, dest):
        return pltpu.make_async_remote_copy(
            src_ref=db.at[NR - 1, :, cols(j)], dst_ref=dz.at[c], send_sem=e_s.at[j], recv_sem=e_r.at[0],
            device_id=(r, 4 * j + dest), device_id_type=MESH)

    def d_recv(g):
        part = db.at[pl.ds(0, NR - 1), :, d_cols(g)]
        pltpu.make_async_copy(part, part, d_r.at[g]).wait()

    def e_send(j):
        for dest in range(4):
            @pl.when(c != 4 * j + dest)
            def _():
                e_copy(j, dest).start()

    def d_finish(g):
        d_recv(g)
        total = dp[r, :, d_cols(g)]
        for k in range(NR - 1):
            total += db[k, :, d_cols(g)]
        db[NR - 1, :, d_cols(g)] = total
        for i, j in enumerate(GROUPS[g]):
            e_send(j)

            @pl.when((c >> 2) == j)
            def _():
                dz[c] = total[:, i * WC:(i + 1) * WC]

    def e_sent(j):
        pltpu.make_async_copy(dz.at[pl.ds(0, 3)], dz.at[pl.ds(0, 3)], e_s.at[j]).wait()

        @pl.when((c >> 2) != j)
        def _():
            pltpu.make_async_copy(dz.at[0], dz.at[0], e_s.at[j]).wait()

    def e_recv():
        part = dz.at[pl.ds(0, NP - 1)]
        pltpu.make_async_copy(part, part, e_r.at[0]).wait()

    def early(j):
        split_f(j, 0)
        product(j, 0, 0)
        product(j, 1, 0)

    def late(j):
        split_f(j, 1)
        product(j, 0, 1)
        ex_send(j)
        product(j, 1, 1)

    def exchanged(j):
        ex_recv(j)
        add_exchanged(j)
        z_first(j)

    def split_first():
        a_wait(0, PRE)
        split_a(0, PRE)

    pl.when(jnp.logical_not(is_root))(split_first)
    pl.semaphore_wait(barrier, NR - 1 + NP - 1)
    pl.when(is_root)(root_send)
    pl.when(is_root)(split_first)

    @pl.loop(0, 10)
    def _(n):
        relay(n)

        @pl.when(n < NP - PRE)
        def _():
            a_wait(n + PRE, n + PRE + 1)
            split_a(n + PRE, n + PRE + 1)

        @pl.when(n == NP - PRE)
        def _():
            for zz in range(NZ):
                f_load(zz).wait()
            transpose_f()

    relay(10)
    early(0)
    relay(11)
    relay(12)
    early(1)
    relay(13)
    late(0)
    relay(14)
    early(2)
    exchanged(0)
    relay(15)
    late(1)
    relay(16)
    early(3)
    exchanged(1)
    relay(17)
    late(2)
    diag_product(0)
    relay(18)
    exchanged(2)
    z_second(0)
    diag_product(1)
    z_second(1)
    diag_product(2)
    d_send(0)
    relay(19)
    late(3)
    exchanged(3)
    diag_product(3)
    d_send(1)
    z_second(2)
    tree_sent()
    d_finish(0)
    d_finish(1)
    z_second(3)
    z_finish(0)
    z_finish(1)
    z_finish(2)
    for j in range(NCH):
        ex_sent(j)
        z_sent(j)
    z_finish(3)
    for j in range(NCH):
        e_sent(j)
    for g in range(2):
        d_sent(g)
    e_recv()
    total = dz[0]
    for k in range(1, NP):
        total += dz[k]
    d_ref[...] = total


def local(inverse_tiles, factor_rows, diag_inverse, pattern):
    c = lax.axis_index("pcol")
    dma = pltpu.SemaphoreType.DMA
    col, d = pl.pallas_call(
        kernel,
        out_shape=(jax.ShapeDtypeStruct((SH, W), F32), jax.ShapeDtypeStruct((DR, WC), F32)),
        in_specs=[
            pl.BlockSpec(memory_space=pltpu.SMEM),
            pl.BlockSpec(memory_space=pl.ANY),
            pl.BlockSpec(memory_space=pl.ANY),
        ],
        out_specs=(pl.BlockSpec(memory_space=pltpu.VMEM), pl.BlockSpec(memory_space=pltpu.VMEM)),
        scratch_shapes=[
            pltpu.VMEM((NP, SH, TILE), F32),
            pltpu.VMEM((TILE, TILE), BF16),
            pltpu.VMEM((TILE, TILE), BF16),
            pltpu.VMEM((NZ, SH, W), F32),
            pltpu.VMEM((NCH, TILE, WC), F32),
            pltpu.VMEM((TILE, 2 * WC), BF16),
            pltpu.VMEM((NCH, 2, NZ, SH, WC), F32),
            pltpu.VMEM((NCH, NZ, SH, WC), F32),
            pltpu.VMEM((NCH, 8, SH, WC), F32),
            pltpu.VMEM((NR, DR, W), F32),
            pltpu.VMEM((NR, DR, W), F32),
            pltpu.VMEM((NP, DR, WC), F32),
            pltpu.VMEM((W, NZ * SH), BF16),
            pltpu.VMEM((W, NZ * SH), BF16),
            pltpu.VMEM((NZ * SH, 2 * WC), BF16),
            dma((NP,)), dma((NZ,)),
            dma((NCH,)), dma((4, 4)), dma((4, NS)),
            dma((NCH,)), dma((NCH,)),
            dma((NCH,)), dma((NCH, 2)),
            dma((2,)), dma((2,)),
            dma((NCH,)), dma((1,)),
        ],
        compiler_params=pltpu.CompilerParams(collective_id=1, has_side_effects=True, vmem_limit_bytes=60 << 20),
        name="selected_inversion",
    )(pattern, inverse_tiles.reshape(NP, SH, TILE), factor_rows)
    mine = lax.dynamic_slice_in_dim(d, (c % 4) * DR, DR, 1)
    return -col, diag_inverse + mine


def solution(mesh):
    return jax.shard_map(
        local,
        mesh=mesh,
        in_specs=(P("prow", "pcol"), P("prow", None), P("prow", "pcol"), P()),
        out_specs=(P(("prow", "pcol"), None), P("prow", "pcol")),
        check_vma=False,
    )
```

```python
import jax
import jax.numpy as jnp
from jax import lax
from jax.experimental import pallas as pl
from jax.experimental.pallas import tpu as pltpu
from jax.sharding import PartitionSpec as P

MESH = pl.DeviceIdType.MESH
F32 = jnp.float32
BF16 = jnp.bfloat16

BLK = 128
NX, NY, NZ, NC = 4, 4, 8, 2
NR = NX * NY
NP = NZ * NC
TILE = 1536
SH = TILE // NP
HP = SH // 2
W = 512
WC = 128
NCH = W // WC
DR = W // NR


DIRS = ((1, 0), (3, 0), (0, 1), (0, 3))
SEND = ((57344, 24321, 12544, 4352), (4017, 224, 560, 16), (8, 32776, 34944, 52429), (70, 8198, 17479, 8736))
DEPTH = ((23130, 60186, 1252), (23130, 7146, 58372), (23130, 55510, 10016), (23130, 29308, 36224))
QR = TILE // 4
NSUB = 2
SR = QR // NSUB
NS = NCH * NSUB
HOP = 3
PRE = 7
GROUPS = ((0, 1, 2), (3,))
ZCOPIES = (
    (-1, -3, 0, SH), (-2, -4, 0, HP), (1, 3, 0, SH), (2, 4, HP, HP),
    (-1, -1, 0, SH), (1, 1, 0, SH), (-2, -2, 0, SH), (2, 2, 0, SH),
)
XYORDER = ((2, 2), (1, 0), (3, 0), (0, 1), (0, 3), (1, 1), (3, 3), (1, 3), (3, 1), (2, 0), (0, 2), (2, 1), (1, 2), (2, 3), (3, 2))


def split(v):
    hi = v.astype(BF16)
    lo = (v - hi.astype(F32)).astype(BF16)
    return hi, lo


def kernel(
    pat, a_hbm, f_hbm, col_ref, d_ref,
    a32, ahi, alo, fown, fc, fs, pb, xb, zb, dp, db, dz, fthi, ftlo, qs,
    a_sem, f_sem, own_s, t_s, t_r, x_s, x_r, z_s, z_r, d_s, d_r, e_s, e_r,
):
    r = lax.axis_index("prow")
    c = lax.axis_index("pcol")
    x, y = r >> 2, r & (NY - 1)
    z, core = c >> 1, c & (NC - 1)
    is_root = r == c

    def share_of(s):
        h, zz = s >> 3, s & (NZ - 1)
        dest_core = jnp.where(h == 0, 1 - core, core)
        return NC * zz + dest_core

    def f_load(s):
        return pltpu.make_async_copy(f_hbm.at[pl.ds(pl.multiple_of((NC * s + core) * SH, 8), SH)], fown.at[s], f_sem.at[s])

    def a_load(s):
        return pltpu.make_async_copy(a_hbm.at[share_of(s)], a32.at[s], a_sem.at[s])

    def root_load(j):
        return pltpu.make_async_copy(f_hbm.at[:, cols(j)], fc.at[j], own_s.at[j])

    def cols(j):
        return pl.ds(j * WC, WC)

    @pl.when(is_root)
    def _():
        for j in range(NCH):
            root_load(j).start()

    @pl.loop(0, NP)
    def _(s):
        a_load(s).start()

    for zz in range(NZ):
        f_load(zz).start()

    barrier = pltpu.get_barrier_semaphore()
    for dx, dy in XYORDER:
        pl.semaphore_signal(
            barrier, inc=1, device_id=(((x + dx) & (NX - 1)) * NY + ((y + dy) & (NY - 1)), c), device_id_type=MESH)

    @pl.loop(1, NP)
    def _(k):
        pl.semaphore_signal(barrier, inc=1, device_id=(r, (c + k) & (NP - 1)), device_id_type=MESH)

    root_x, root_y = c >> 2, c & (NY - 1)
    pos = ((x - root_x + NX) & (NX - 1)) * NY + ((y - root_y + NY) & (NY - 1))
    depth = [sum(((DEPTH[t][k] >> pos) & 1) << k for k in range(3)) for t in range(4)]
    sends = [[(SEND[t][d] >> pos) & 1 for d in range(4)] for t in range(4)]
    rank = [sum((((depth[u] < depth[t]) | ((depth[u] == depth[t]) & (u < t))).astype(jnp.int32) for u in range(4) if u != t), 0) for t in range(4)]
    order = [sum(t * (rank[t] == k).astype(jnp.int32) for t in range(4)) for k in range(4)]
    peers = [(((x + dx) & (NX - 1)) * NY + ((y + dy) & (NY - 1)), c) for dx, dy in DIRS]

    def piece(t, s):
        return fc.at[s >> 1, pl.ds(pl.multiple_of(t * QR + (s & (NSUB - 1)) * SR, 8), SR)]

    def tree_copy(t, s, d):
        return pltpu.make_async_remote_copy(
            src_ref=piece(t, s), dst_ref=piece(t, s), send_sem=t_s.at[t, d], recv_sem=t_r.at[t, s],
            device_id=peers[d], device_id_type=MESH)

    def tree_send(t, s):
        for d in range(4):
            @pl.when(sends[t][d] == 1)
            def _():
                tree_copy(t, s, d).start()

    def relay(n):
        for t in range(4):
            s = jnp.where(is_root, n, n - HOP * (depth[t] - 1))

            @pl.when((s >= 0) & (s < NS))
            def _():
                @pl.when(jnp.logical_not(is_root))
                def _():
                    pltpu.make_async_copy(piece(t, s), piece(t, s), t_r.at[t, s]).wait()
                tree_send(t, s)

    def tree_sent():
        for t in range(4):
            part = fc.at[:, pl.ds(t * QR, QR)]
            for d in range(4):
                @pl.when(sends[t][d] == 1)
                def _():
                    pltpu.make_async_copy(part, part, t_s.at[t, d]).wait()

    def split_a(first, last):
        @pl.loop(first, last)
        def _(s):
            for k in range(4):
                hi, lo = split(a32[s, :, pl.ds(pl.multiple_of(order[k] * QR, 128), QR)])
                at = (pl.ds(pl.multiple_of(s * SH, 16), SH), pl.ds(k * QR, QR))
                ahi[at] = hi
                alo[at] = lo

    def a_wait(first, last):
        @pl.loop(first, last)
        def _(s):
            a_load(s).wait()

    def transpose_f():
        for g in range(2):
            masks = []
            for q in range(12):
                row = r * TILE + SH * (NC * (4 * g + q // 3) + core) + 32 * (q % 3)
                masks.append(pat[row >> 7].astype(F32))
            for cb in range(W // 128):
                v = fown[pl.ds(4 * g, 4), :, pl.ds(cb * 128, 128)].reshape(4 * SH, 128)
                for b in range(3):
                    part = jnp.concatenate(
                        [v[128 * b + 32 * q: 128 * b + 32 * q + 32] * masks[4 * b + q] for q in range(4)], axis=0)
                    hi, lo = split(part.T)
                    at = (pl.ds(cb * 128, 128), pl.ds((3 * g + b) * 128, 128))
                    fthi[at] = hi
                    ftlo[at] = lo

    def split_f(j, pair):
        for k in (2 * pair, 2 * pair + 1):
            for b in range(QR // BLK):
                rows = pl.ds(pl.multiple_of(order[k] * QR + b * BLK, BLK), BLK)
                hi, lo = split(fc[j, rows] * pat[c * (TILE // BLK) + order[k] * (QR // BLK) + b].astype(F32))
                rows = pl.ds(k * QR + b * BLK, BLK)
                fs[rows, 0:WC] = hi
                fs[rows, WC:2 * WC] = lo

    def product(j, h, pair):
        rows, depths = pl.ds(h * NZ * SH, NZ * SH), pl.ds(pair * 2 * QR, 2 * QR)
        p = jnp.dot(ahi[rows, depths], fs[depths, :], preferred_element_type=F32)
        q = jnp.dot(alo[rows, depths], fs[depths, 0:WC], preferred_element_type=F32)
        v = (p[:, 0:WC] + (p[:, WC:2 * WC] + q)).reshape(NZ, SH, WC)
        pb[j, h] = v if pair == 0 else pb[j, h] + v

    def exchange(j):
        return pltpu.make_async_remote_copy(
            src_ref=pb.at[j, 0], dst_ref=xb.at[j], send_sem=x_s.at[j], recv_sem=x_r.at[j],
            device_id=(r, c + 1 - 2 * core), device_id_type=MESH)

    def ex_send(j):
        exchange(j).start()

    def ex_recv(j):
        exchange(j).wait_recv()

    def ex_sent(j):
        exchange(j).wait_send()

    def add_exchanged(j):
        @pl.loop(0, NZ)
        def _(zz):
            v = pb[j, 1, zz] + xb[j, zz]
            pb[j, 1, zz] = v

    def z_copy(j, slot):
        away, off, first, count = ZCOPIES[slot]
        rows = pl.ds(first, count)
        return pltpu.make_async_remote_copy(
            src_ref=pb.at[j, 1, (z + off + NZ) & (NZ - 1), rows], dst_ref=zb.at[j, slot, rows],
            send_sem=z_s.at[j], recv_sem=z_r.at[j, slot // 4],
            device_id=(r, (c + NC * away + NP) & (NP - 1)), device_id_type=MESH)

    def z_send(j, slot):
        z_copy(j, slot).start()

    def z_recv(j, stage):
        part = zb.at[j, pl.ds(4 * stage, 3 + stage)]
        pltpu.make_async_copy(part, part, z_r.at[j, stage]).wait()

    def z_sent(j):
        part = zb.at[j, pl.ds(0, 7)]
        pltpu.make_async_copy(part, part, z_s.at[j]).wait()

    def z_add(j):
        for slot in range(4):
            _, _, first, count = ZCOPIES[slot]
            share, rows = (z + (NZ - 2 if slot < 2 else 2)) & (NZ - 1), pl.ds(first, count)
            pb[j, 1, share, rows] = pb[j, 1, share, rows] + zb[j, slot, rows]

    def z_first(j):
        for slot in (1, 3, 0, 2, 4, 5):
            z_send(j, slot)

    def z_second(j):
        z_recv(j, 0)
        z_add(j)
        for slot in (6, 7):
            z_send(j, slot)

    def z_finish(j):
        z_recv(j, 1)
        total = pb[j, 1, z] + ((zb[j, 4] + zb[j, 5]) + (zb[j, 6] + zb[j, 7]))
        for q in range(3):
            row = r * TILE + SH * c + 32 * q
            col_ref[pl.ds(32 * q, 32), cols(j)] = total[32 * q:32 * q + 32] * pat[row >> 7].astype(F32)

    def diag_product(j):
        for g in range(2):
            v = pb[j, 1, pl.ds(4 * g, 4)].reshape(4 * SH, WC)
            hi, lo = split(v)
            qs[pl.ds(g * 4 * SH, 4 * SH), 0:WC] = hi
            qs[pl.ds(g * 4 * SH, 4 * SH), WC:2 * WC] = lo
        p = jnp.dot(fthi[...], qs[...], preferred_element_type=F32)
        q = jnp.dot(ftlo[...], qs[:, 0:WC], preferred_element_type=F32)
        dp[:, :, cols(j)] = (p[:, 0:WC] + (p[:, WC:2 * WC] + q)).reshape(NR, DR, WC)

    def d_cols(g):
        return pl.ds(GROUPS[g][0] * WC, len(GROUPS[g]) * WC)

    def d_send(g):
        for k, (dx, dy) in enumerate(XYORDER, 1):
            to = ((x + dx) & (NX - 1)) * NY + ((y + dy) & (NY - 1))
            pltpu.make_async_remote_copy(
                src_ref=dp.at[to, :, d_cols(g)], dst_ref=db.at[k - 1, :, d_cols(g)],
                send_sem=d_s.at[g], recv_sem=d_r.at[g],
                device_id=(to, c), device_id_type=MESH).start()

    def d_sent(g):
        part = dp.at[pl.ds(0, NR - 1), :, d_cols(g)]
        pltpu.make_async_copy(part, part, d_s.at[g]).wait()

    def e_copy(j, dest):
        return pltpu.make_async_remote_copy(
            src_ref=db.at[NR - 1, :, cols(j)], dst_ref=dz.at[c], send_sem=e_s.at[j], recv_sem=e_r.at[0],
            device_id=(r, 4 * j + dest), device_id_type=MESH)

    def d_recv(g):
        part = db.at[pl.ds(0, NR - 1), :, d_cols(g)]
        pltpu.make_async_copy(part, part, d_r.at[g]).wait()

    def e_send(j):
        for dest in range(4):
            @pl.when(c != 4 * j + dest)
            def _():
                e_copy(j, dest).start()

    def d_finish(g):
        d_recv(g)
        total = dp[r, :, d_cols(g)]
        for k in range(NR - 1):
            total += db[k, :, d_cols(g)]
        db[NR - 1, :, d_cols(g)] = total
        for i, j in enumerate(GROUPS[g]):
            e_send(j)

            @pl.when((c >> 2) == j)
            def _():
                dz[c] = total[:, i * WC:(i + 1) * WC]

    def e_sent(j):
        pltpu.make_async_copy(dz.at[pl.ds(0, 3)], dz.at[pl.ds(0, 3)], e_s.at[j]).wait()

        @pl.when((c >> 2) != j)
        def _():
            pltpu.make_async_copy(dz.at[0], dz.at[0], e_s.at[j]).wait()

    def e_recv():
        part = dz.at[pl.ds(0, NP - 1)]
        pltpu.make_async_copy(part, part, e_r.at[0]).wait()

    def early(j):
        split_f(j, 0)
        product(j, 0, 0)
        product(j, 1, 0)

    def late(j):
        split_f(j, 1)
        product(j, 0, 1)
        ex_send(j)
        product(j, 1, 1)

    def exchanged(j):
        ex_recv(j)
        add_exchanged(j)
        z_first(j)

    a_wait(0, PRE)
    split_a(0, PRE)
    pl.semaphore_wait(barrier, NR - 1 + NP - 1)

    @pl.when(is_root)
    def _():
        for j in range(NCH):
            root_load(j).wait()

    @pl.loop(0, 10)
    def _(n):
        relay(n)

        @pl.when(n < NP - PRE)
        def _():
            a_wait(n + PRE, n + PRE + 1)
            split_a(n + PRE, n + PRE + 1)

        @pl.when(n == NP - PRE)
        def _():
            for zz in range(NZ):
                f_load(zz).wait()
            transpose_f()

    relay(10)
    early(0)
    relay(11)
    relay(12)
    early(1)
    relay(13)
    late(0)
    relay(14)
    early(2)
    exchanged(0)
    relay(15)
    late(1)
    relay(16)
    early(3)
    exchanged(1)
    relay(17)
    late(2)
    diag_product(0)
    relay(18)
    exchanged(2)
    z_second(0)
    diag_product(1)
    z_second(1)
    diag_product(2)
    d_send(0)
    relay(19)
    late(3)
    exchanged(3)
    diag_product(3)
    d_send(1)
    z_second(2)
    z_second(3)
    tree_sent()
    d_finish(0)
    z_finish(0)
    d_finish(1)
    z_finish(1)
    z_finish(2)
    for j in range(NCH):
        ex_sent(j)
        z_sent(j)
    z_finish(3)
    for j in range(NCH):
        e_sent(j)
    for g in range(2):
        d_sent(g)
    e_recv()
    total = dz[0]
    for k in range(1, NP):
        total += dz[k]
    d_ref[...] = total


def local(inverse_tiles, factor_rows, diag_inverse, pattern):
    c = lax.axis_index("pcol")
    dma = pltpu.SemaphoreType.DMA
    col, d = pl.pallas_call(
        kernel,
        out_shape=(jax.ShapeDtypeStruct((SH, W), F32), jax.ShapeDtypeStruct((DR, WC), F32)),
        in_specs=[
            pl.BlockSpec(memory_space=pltpu.SMEM),
            pl.BlockSpec(memory_space=pl.ANY),
            pl.BlockSpec(memory_space=pl.ANY),
        ],
        out_specs=(pl.BlockSpec(memory_space=pltpu.VMEM), pl.BlockSpec(memory_space=pltpu.VMEM)),
        scratch_shapes=[
            pltpu.VMEM((NP, SH, TILE), F32),
            pltpu.VMEM((TILE, TILE), BF16),
            pltpu.VMEM((TILE, TILE), BF16),
            pltpu.VMEM((NZ, SH, W), F32),
            pltpu.VMEM((NCH, TILE, WC), F32),
            pltpu.VMEM((TILE, 2 * WC), BF16),
            pltpu.VMEM((NCH, 2, NZ, SH, WC), F32),
            pltpu.VMEM((NCH, NZ, SH, WC), F32),
            pltpu.VMEM((NCH, 8, SH, WC), F32),
            pltpu.VMEM((NR, DR, W), F32),
            pltpu.VMEM((NR, DR, W), F32),
            pltpu.VMEM((NP, DR, WC), F32),
            pltpu.VMEM((W, NZ * SH), BF16),
            pltpu.VMEM((W, NZ * SH), BF16),
            pltpu.VMEM((NZ * SH, 2 * WC), BF16),
            dma((NP,)), dma((NZ,)),
            dma((NCH,)), dma((4, 4)), dma((4, NS)),
            dma((NCH,)), dma((NCH,)),
            dma((NCH,)), dma((NCH, 2)),
            dma((2,)), dma((2,)),
            dma((NCH,)), dma((1,)),
        ],
        compiler_params=pltpu.CompilerParams(collective_id=1, has_side_effects=True, vmem_limit_bytes=60 << 20),
        name="selected_inversion",
    )(pattern, inverse_tiles.reshape(NP, SH, TILE), factor_rows)
    mine = lax.dynamic_slice_in_dim(d, (c % 4) * DR, DR, 1)
    return -col, diag_inverse + mine


def solution(mesh):
    return jax.shard_map(
        local,
        mesh=mesh,
        in_specs=(P("prow", "pcol"), P("prow", None), P("prow", "pcol"), P()),
        out_specs=(P(("prow", "pcol"), None), P("prow", "pcol")),
        check_vma=False,
    )
```

```python
import jax
import jax.numpy as jnp
from jax import lax
from jax.experimental import pallas as pl
from jax.experimental.pallas import tpu as pltpu
from jax.sharding import PartitionSpec as P

MESH = pl.DeviceIdType.MESH
F32 = jnp.float32
BF16 = jnp.bfloat16

BLK = 128
NX, NY, NZ, NC = 4, 4, 8, 2
NR = NX * NY
NP = NZ * NC
TILE = 1536
SH = TILE // NP
HP = SH // 2
W = 512
WC = 128
NCH = W // WC
DR = W // NR


DIRS = ((1, 0), (3, 0), (0, 1), (0, 3))
SEND = ((57344, 24321, 12544, 4352), (4017, 224, 560, 16), (8, 32776, 34944, 52429), (70, 8198, 17479, 8736))
DEPTH = ((23130, 60186, 1252), (23130, 7146, 58372), (23130, 55510, 10016), (23130, 29308, 36224))
QR = TILE // 4
NSUB = 2
SR = QR // NSUB
NS = NCH * NSUB
HOP = 3
PRE = 7
GROUPS = ((0, 1, 2), (3,))
ZCOPIES = (
    (-1, -3, 0, SH), (-2, -4, 0, HP), (1, 3, 0, SH), (2, 4, HP, HP),
    (-1, -1, 0, SH), (1, 1, 0, SH), (-2, -2, 0, SH), (2, 2, 0, SH),
)
XYORDER = ((2, 2), (1, 0), (3, 0), (0, 1), (0, 3), (1, 1), (3, 3), (1, 3), (3, 1), (2, 0), (0, 2), (2, 1), (1, 2), (2, 3), (3, 2))


def split(v):
    hi = v.astype(BF16)
    lo = (v - hi.astype(F32)).astype(BF16)
    return hi, lo


def kernel(
    pat, a_hbm, f_hbm, col_ref, d_ref,
    a32, ahi, alo, fown, fc, fs, pb, xb, zb, dp, db, dz, fthi, ftlo, qs,
    a_sem, f_sem, own_s, t_s, t_r, x_s, x_r, z_s, z_r, d_s, d_r, e_s, e_r,
):
    r = lax.axis_index("prow")
    c = lax.axis_index("pcol")
    x, y = r // NY, r % NY
    z, core = c // NC, c % NC
    is_root = r == c

    def share_of(s):
        h, zz = s // NZ, s % NZ
        dest_core = jnp.where(h == 0, 1 - core, core)
        return NC * zz + dest_core

    def f_load(s):
        return pltpu.make_async_copy(f_hbm.at[pl.ds(pl.multiple_of((NC * s + core) * SH, 8), SH)], fown.at[s], f_sem.at[s])

    def a_load(s):
        return pltpu.make_async_copy(a_hbm.at[share_of(s)], a32.at[s], a_sem.at[s])

    def root_load(j):
        return pltpu.make_async_copy(f_hbm.at[:, cols(j)], fc.at[j], own_s.at[j])

    def cols(j):
        return pl.ds(j * WC, WC)

    @pl.when(is_root)
    def _():
        for j in range(NCH):
            root_load(j).start()

    @pl.loop(0, NP)
    def _(s):
        a_load(s).start()

    for zz in range(NZ):
        f_load(zz).start()

    barrier = pltpu.get_barrier_semaphore()
    for dx, dy in XYORDER:
        pl.semaphore_signal(
            barrier, inc=1, device_id=((x + dx) % NX * NY + (y + dy) % NY, c), device_id_type=MESH)

    @pl.loop(1, NP)
    def _(k):
        pl.semaphore_signal(barrier, inc=1, device_id=(r, (c + k) % NP), device_id_type=MESH)

    root_x, root_y = c // NY, c % NY
    pos = (x - root_x + NX) % NX * NY + (y - root_y + NY) % NY
    depth = [sum(((DEPTH[t][k] >> pos) & 1) << k for k in range(3)) for t in range(4)]
    sends = [[(SEND[t][d] >> pos) & 1 for d in range(4)] for t in range(4)]
    rank = [sum((((depth[u] < depth[t]) | ((depth[u] == depth[t]) & (u < t))).astype(jnp.int32) for u in range(4) if u != t), 0) for t in range(4)]
    order = [sum(t * (rank[t] == k).astype(jnp.int32) for t in range(4)) for k in range(4)]
    peers = [((x + dx) % NX * NY + (y + dy) % NY, c) for dx, dy in DIRS]

    def piece(t, s):
        return fc.at[s // NSUB, pl.ds(pl.multiple_of(t * QR + (s % NSUB) * SR, 8), SR)]

    def tree_copy(t, s, d):
        return pltpu.make_async_remote_copy(
            src_ref=piece(t, s), dst_ref=piece(t, s), send_sem=t_s.at[t, d], recv_sem=t_r.at[t, s],
            device_id=peers[d], device_id_type=MESH)

    def tree_send(t, s):
        for d in range(4):
            @pl.when(sends[t][d] == 1)
            def _():
                tree_copy(t, s, d).start()

    def relay(n):
        for t in range(4):
            s = jnp.where(is_root, n, n - HOP * (depth[t] - 1))

            @pl.when((s >= 0) & (s < NS))
            def _():
                @pl.when(jnp.logical_not(is_root))
                def _():
                    pltpu.make_async_copy(piece(t, s), piece(t, s), t_r.at[t, s]).wait()
                tree_send(t, s)

    def tree_sent():
        for t in range(4):
            part = fc.at[:, pl.ds(t * QR, QR)]
            for d in range(4):
                @pl.when(sends[t][d] == 1)
                def _():
                    pltpu.make_async_copy(part, part, t_s.at[t, d]).wait()

    def split_a(first, last):
        @pl.loop(first, last)
        def _(s):
            for k in range(4):
                hi, lo = split(a32[s, :, pl.ds(pl.multiple_of(order[k] * QR, 128), QR)])
                at = (pl.ds(pl.multiple_of(s * SH, 16), SH), pl.ds(k * QR, QR))
                ahi[at] = hi
                alo[at] = lo

    def a_wait(first, last):
        @pl.loop(first, last)
        def _(s):
            a_load(s).wait()

    def transpose_f():
        for g in range(2):
            masks = []
            for q in range(12):
                row = r * TILE + SH * (NC * (4 * g + q // 3) + core) + 32 * (q % 3)
                masks.append(pat[row // BLK].astype(F32))
            for cb in range(W // 128):
                v = fown[pl.ds(4 * g, 4), :, pl.ds(cb * 128, 128)].reshape(4 * SH, 128)
                for b in range(3):
                    part = jnp.concatenate(
                        [v[128 * b + 32 * q: 128 * b + 32 * q + 32] * masks[4 * b + q] for q in range(4)], axis=0)
                    hi, lo = split(part.T)
                    at = (pl.ds(cb * 128, 128), pl.ds((3 * g + b) * 128, 128))
                    fthi[at] = hi
                    ftlo[at] = lo

    def split_f(j, pair):
        for k in (2 * pair, 2 * pair + 1):
            for b in range(QR // BLK):
                rows = pl.ds(pl.multiple_of(order[k] * QR + b * BLK, BLK), BLK)
                hi, lo = split(fc[j, rows] * pat[c * (TILE // BLK) + order[k] * (QR // BLK) + b].astype(F32))
                rows = pl.ds(k * QR + b * BLK, BLK)
                fs[rows, 0:WC] = hi
                fs[rows, WC:2 * WC] = lo

    def product(j, h, pair):
        rows, depths = pl.ds(h * NZ * SH, NZ * SH), pl.ds(pair * 2 * QR, 2 * QR)
        p = jnp.dot(ahi[rows, depths], fs[depths, :], preferred_element_type=F32)
        q = jnp.dot(alo[rows, depths], fs[depths, 0:WC], preferred_element_type=F32)
        v = (p[:, 0:WC] + (p[:, WC:2 * WC] + q)).reshape(NZ, SH, WC)
        pb[j, h] = v if pair == 0 else pb[j, h] + v

    def exchange(j):
        return pltpu.make_async_remote_copy(
            src_ref=pb.at[j, 0], dst_ref=xb.at[j], send_sem=x_s.at[j], recv_sem=x_r.at[j],
            device_id=(r, c + 1 - 2 * core), device_id_type=MESH)

    def ex_send(j):
        exchange(j).start()

    def ex_recv(j):
        exchange(j).wait_recv()

    def ex_sent(j):
        exchange(j).wait_send()

    def add_exchanged(j):
        @pl.loop(0, NZ)
        def _(zz):
            v = pb[j, 1, zz] + xb[j, zz]
            pb[j, 1, zz] = v

    def z_copy(j, slot):
        away, off, first, count = ZCOPIES[slot]
        rows = pl.ds(first, count)
        return pltpu.make_async_remote_copy(
            src_ref=pb.at[j, 1, (z + off + NZ) % NZ, rows], dst_ref=zb.at[j, slot, rows],
            send_sem=z_s.at[j], recv_sem=z_r.at[j, slot // 4],
            device_id=(r, (c + NC * away + NP) % NP), device_id_type=MESH)

    def z_send(j, slot):
        z_copy(j, slot).start()

    def z_recv(j, stage):
        part = zb.at[j, pl.ds(4 * stage, 3 + stage)]
        pltpu.make_async_copy(part, part, z_r.at[j, stage]).wait()

    def z_sent(j):
        part = zb.at[j, pl.ds(0, 7)]
        pltpu.make_async_copy(part, part, z_s.at[j]).wait()

    def z_add(j):
        for slot in range(4):
            _, _, first, count = ZCOPIES[slot]
            share, rows = (z + (NZ - 2 if slot < 2 else 2)) % NZ, pl.ds(first, count)
            pb[j, 1, share, rows] = pb[j, 1, share, rows] + zb[j, slot, rows]

    def z_first(j):
        for slot in (1, 3, 0, 2, 4, 5):
            z_send(j, slot)

    def z_second(j):
        z_recv(j, 0)
        z_add(j)
        for slot in (6, 7):
            z_send(j, slot)

    def z_finish(j):
        z_recv(j, 1)
        total = pb[j, 1, z] + ((zb[j, 4] + zb[j, 5]) + (zb[j, 6] + zb[j, 7]))
        for q in range(3):
            row = r * TILE + SH * c + 32 * q
            col_ref[pl.ds(32 * q, 32), cols(j)] = total[32 * q:32 * q + 32] * pat[row // BLK].astype(F32)

    def diag_product(j):
        for g in range(2):
            v = pb[j, 1, pl.ds(4 * g, 4)].reshape(4 * SH, WC)
            hi, lo = split(v)
            qs[pl.ds(g * 4 * SH, 4 * SH), 0:WC] = hi
            qs[pl.ds(g * 4 * SH, 4 * SH), WC:2 * WC] = lo
        p = jnp.dot(fthi[...], qs[...], preferred_element_type=F32)
        q = jnp.dot(ftlo[...], qs[:, 0:WC], preferred_element_type=F32)
        dp[:, :, cols(j)] = (p[:, 0:WC] + (p[:, WC:2 * WC] + q)).reshape(NR, DR, WC)

    def d_cols(g):
        return pl.ds(GROUPS[g][0] * WC, len(GROUPS[g]) * WC)

    def d_send(g):
        for k, (dx, dy) in enumerate(XYORDER, 1):
            to = (x + dx) % NX * NY + (y + dy) % NY
            pltpu.make_async_remote_copy(
                src_ref=dp.at[to, :, d_cols(g)], dst_ref=db.at[k - 1, :, d_cols(g)],
                send_sem=d_s.at[g], recv_sem=d_r.at[g],
                device_id=(to, c), device_id_type=MESH).start()

    def d_sent(g):
        part = dp.at[pl.ds(0, NR - 1), :, d_cols(g)]
        pltpu.make_async_copy(part, part, d_s.at[g]).wait()

    def e_copy(j, dest):
        return pltpu.make_async_remote_copy(
            src_ref=db.at[NR - 1, :, cols(j)], dst_ref=dz.at[c], send_sem=e_s.at[j], recv_sem=e_r.at[0],
            device_id=(r, 4 * j + dest), device_id_type=MESH)

    def d_recv(g):
        part = db.at[pl.ds(0, NR - 1), :, d_cols(g)]
        pltpu.make_async_copy(part, part, d_r.at[g]).wait()

    def e_send(j):
        for dest in range(4):
            @pl.when(c != 4 * j + dest)
            def _():
                e_copy(j, dest).start()

    def d_finish(g):
        d_recv(g)
        total = dp[r, :, d_cols(g)]
        for k in range(NR - 1):
            total += db[k, :, d_cols(g)]
        db[NR - 1, :, d_cols(g)] = total
        for i, j in enumerate(GROUPS[g]):
            e_send(j)

            @pl.when(c // 4 == j)
            def _():
                dz[c] = total[:, i * WC:(i + 1) * WC]

    def e_sent(j):
        pltpu.make_async_copy(dz.at[pl.ds(0, 3)], dz.at[pl.ds(0, 3)], e_s.at[j]).wait()

        @pl.when(c // 4 != j)
        def _():
            pltpu.make_async_copy(dz.at[0], dz.at[0], e_s.at[j]).wait()

    def e_recv():
        part = dz.at[pl.ds(0, NP - 1)]
        pltpu.make_async_copy(part, part, e_r.at[0]).wait()

    def early(j):
        split_f(j, 0)
        product(j, 0, 0)
        product(j, 1, 0)

    def late(j):
        split_f(j, 1)
        product(j, 0, 1)
        ex_send(j)
        product(j, 1, 1)

    def exchanged(j):
        ex_recv(j)
        add_exchanged(j)
        z_first(j)

    a_wait(0, PRE)
    split_a(0, PRE)
    pl.semaphore_wait(barrier, NR - 1 + NP - 1)

    @pl.when(is_root)
    def _():
        for j in range(NCH):
            root_load(j).wait()

    @pl.loop(0, 10)
    def _(n):
        relay(n)

        @pl.when(n < NP - PRE)
        def _():
            a_wait(n + PRE, n + PRE + 1)
            split_a(n + PRE, n + PRE + 1)

        @pl.when(n == NP - PRE)
        def _():
            for zz in range(NZ):
                f_load(zz).wait()
            transpose_f()

    relay(10)
    early(0)
    relay(11)
    relay(12)
    early(1)
    relay(13)
    late(0)
    relay(14)
    early(2)
    exchanged(0)
    relay(15)
    late(1)
    relay(16)
    early(3)
    exchanged(1)
    relay(17)
    late(2)
    diag_product(0)
    relay(18)
    exchanged(2)
    z_second(0)
    diag_product(1)
    z_second(1)
    diag_product(2)
    d_send(0)
    relay(19)
    late(3)
    exchanged(3)
    diag_product(3)
    d_send(1)
    z_second(2)
    z_second(3)
    tree_sent()
    d_finish(0)
    z_finish(0)
    d_finish(1)
    z_finish(1)
    z_finish(2)
    for j in range(NCH):
        ex_sent(j)
        z_sent(j)
    z_finish(3)
    for j in range(NCH):
        e_sent(j)
    for g in range(2):
        d_sent(g)
    e_recv()
    total = dz[0]
    for k in range(1, NP):
        total += dz[k]
    d_ref[...] = total


def closing(col_ref, d_ref, diag_ref, column_ref, diagonal_ref):
    place = lax.axis_index("pcol") & 3
    mine = d_ref[:, 0:DR]
    for k in range(1, WC // DR):
        mine = jnp.where(place == k, d_ref[:, k * DR:(k + 1) * DR], mine)
    column_ref[...] = -col_ref[...]
    diagonal_ref[...] = diag_ref[...] + mine


def local(inverse_tiles, factor_rows, diag_inverse, pattern):
    dma = pltpu.SemaphoreType.DMA
    col, d = pl.pallas_call(
        kernel,
        out_shape=(jax.ShapeDtypeStruct((SH, W), F32), jax.ShapeDtypeStruct((DR, WC), F32)),
        in_specs=[
            pl.BlockSpec(memory_space=pltpu.SMEM),
            pl.BlockSpec(memory_space=pl.ANY),
            pl.BlockSpec(memory_space=pl.ANY),
        ],
        out_specs=(pl.BlockSpec(memory_space=pltpu.VMEM), pl.BlockSpec(memory_space=pltpu.VMEM)),
        scratch_shapes=[
            pltpu.VMEM((NP, SH, TILE), F32),
            pltpu.VMEM((TILE, TILE), BF16),
            pltpu.VMEM((TILE, TILE), BF16),
            pltpu.VMEM((NZ, SH, W), F32),
            pltpu.VMEM((NCH, TILE, WC), F32),
            pltpu.VMEM((TILE, 2 * WC), BF16),
            pltpu.VMEM((NCH, 2, NZ, SH, WC), F32),
            pltpu.VMEM((NCH, NZ, SH, WC), F32),
            pltpu.VMEM((NCH, 8, SH, WC), F32),
            pltpu.VMEM((NR, DR, W), F32),
            pltpu.VMEM((NR, DR, W), F32),
            pltpu.VMEM((NP, DR, WC), F32),
            pltpu.VMEM((W, NZ * SH), BF16),
            pltpu.VMEM((W, NZ * SH), BF16),
            pltpu.VMEM((NZ * SH, 2 * WC), BF16),
            dma((NP,)), dma((NZ,)),
            dma((NCH,)), dma((4, 4)), dma((4, NS)),
            dma((NCH,)), dma((NCH,)),
            dma((NCH,)), dma((NCH, 2)),
            dma((2,)), dma((2,)),
            dma((NCH,)), dma((1,)),
        ],
        compiler_params=pltpu.CompilerParams(collective_id=1, has_side_effects=True, vmem_limit_bytes=60 << 20),
        name="selected_inversion",
    )(pattern, inverse_tiles.reshape(NP, SH, TILE), factor_rows)
    vmem = pl.BlockSpec(memory_space=pltpu.VMEM)
    return pl.pallas_call(
        closing,
        out_shape=(jax.ShapeDtypeStruct((SH, W), F32), jax.ShapeDtypeStruct((DR, DR), F32)),
        in_specs=[vmem] * 3,
        out_specs=(vmem, vmem),
        name="closing",
    )(col, d, diag_inverse)


def solution(mesh):
    return jax.shard_map(
        local,
        mesh=mesh,
        in_specs=(P("prow", "pcol"), P("prow", None), P("prow", "pcol"), P()),
        out_specs=(P(("prow", "pcol"), None), P("prow", "pcol")),
        check_vma=False,
    )
```
